32 devices in a mesh: stn: 4 (over x, core), tm: 8 (over z, y).
Axes of the slice: x: 2, y: 2, z: 4, core: 2. Of those that a mesh axis runs over, the one named last changes fastest.
Arguments:
- samples: bfloat16 [2, 1024, 8, 20736], P(None, 'stn', 'tm'), may hold values from -22 to 22
- filter_taps: float32 [6, 3456], replicated, may hold values from -2.5 to 2.5
- station_flags: int32 [1024], P('stn'), may hold values 0 or 1
- channel_keep: int32 [3456], replicated, may hold values from 0 to 1, as said below
- beam_delay: int32 [64, 1024], replicated, may hold values from 0 to 3455
Outputs:
- visibilities: float32 [16, 2, 1024, 1024], P(None, None, 'stn', 'tm')
- beam_power: float32 [64, 3456], P('stn', 'tm')
The draws below stay inside these ranges and needn't reach their ends.
Inputs may be any that keep to these rules, and one draw needn't show every extreme that they name: `channel_keep`: each value is 0 or 1, and the first fine channel of every output channel is 1.
All inputs are finite; a program needn't handle non-finite values. No bound on the sum of `station_flags` on one device may be relied on, other than what follows from the above.
Results may differ from the reference program's by a relative error of at most 0.013.
Values may be sent and summed in bfloat16 or wider, within the bound.
A program may use at most 128 MiB of HBM per device.

```python
import math
import jax
import jax.numpy as jnp
from jax import lax

INPUTS = 1024
FINE = 3456
OUTCH = 16
BEAMS = 64
TAPS = 6
SPECTRA = 8
GROUP = 216
SUB = 216


SKY_AMPLITUDES = (1.0, 0.7, 0.5, 0.35)


def draw_samples(key, part):
    window = TAPS * FINE
    signal_key = jax.random.fold_in(key, 11)
    signal = jax.random.truncated_normal(signal_key, -4.0, 4.0, (2, 4, SPECTRA, window), jnp.float32)

    def one_input(input_id):
        input_key = jax.random.fold_in(key, input_id + 100)
        thermal_key, phase_key = jax.random.split(input_key, 2)
        phases = jax.random.uniform(phase_key, (4,), jnp.float32, -math.pi, math.pi)
        thermal = jax.random.truncated_normal(thermal_key, -4.0, 4.0, (2, SPECTRA, window), jnp.float32)
        real_part = thermal[0]
        imag_part = thermal[1]
        for source in range(4):
            cosine = jnp.cos(phases[source])
            sine_value = jnp.sin(phases[source])
            real_part = real_part + SKY_AMPLITUDES[source] * (cosine * signal[0, source] - sine_value * signal[1, source])
            imag_part = imag_part + SKY_AMPLITUDES[source] * (sine_value * signal[0, source] + cosine * signal[1, source])
        return jnp.stack([real_part, imag_part]).astype(jnp.bfloat16)
    values = lax.map(one_input, jnp.arange(INPUTS, dtype=jnp.int32))
    return jnp.moveaxis(values, 0, 1)


def draw_channel_keep(key, part):
    draw_codes = jax.random.randint(key, (FINE,), 0, 8)
    kept_mask = (draw_codes != 0).astype(jnp.int32)
    group_start = jnp.arange(FINE, dtype=jnp.int32) % (FINE // OUTCH) == 0
    return jnp.where(group_start, 1, kept_mask).astype(jnp.int32)


def with_ends(result, stream_key, smallest, high):
    dims = result.shape
    index_at = [jax.random.randint(jax.random.fold_in(stream_key, axis), (), 0, dims[axis]) for axis in range(len(dims))]
    result = result.at[tuple(index_at)].set(smallest)
    longest = dims.index(max(dims))
    index_at[longest] = (index_at[longest] + 1) % dims[longest]
    return result.at[tuple(index_at)].set(high)


def normal_values(rng, dims, spread, bound, kind=jnp.bfloat16):
    entries = spread * jax.random.normal(rng, dims, jnp.float32)
    return jnp.clip(entries, min=-bound, max=bound).astype(kind)


def setup_inputs(seed: int = 0) -> dict:
    key_of = jax.random.split(jax.random.key(seed), 6)
    return {
        "samples": draw_samples(jax.random.fold_in(key_of[5], 71), 0),
        "filter_taps": normal_values(key_of[1], (TAPS, FINE), TAPS ** -0.5, 2.5, jnp.float32),
        "station_flags": with_ends((jax.random.randint(key_of[2], (INPUTS,), 0, 8) < 7).astype(jnp.int32), jax.random.fold_in(key_of[2], 1), 0, 1),
        "channel_keep": draw_channel_keep(jax.random.fold_in(key_of[5], 71), 0),
        "beam_delay": with_ends(jax.random.randint(key_of[4], (BEAMS, INPUTS), 0, FINE), jax.random.fold_in(key_of[4], 1), 0, FINE - 1).astype(jnp.int32),
    }


HIGHEST = lax.Precision.HIGHEST

def reference(samples, filter_taps, station_flags, channel_keep, beam_delay):

    def channelize(input_id):
        framed = samples[:, input_id].astype(jnp.float32).reshape(2, SPECTRA, TAPS, FINE)
        branch = lax.optimization_barrier(jnp.sum(framed * filter_taps[None, None], axis=2))
        transformed = jnp.fft.fft(branch[0] + 1j * branch[1], axis=-1)
        factor = station_flags[input_id].astype(jnp.float32) / math.sqrt(FINE)
        stacked = jnp.stack([jnp.real(transformed), jnp.imag(transformed)]) * factor
        return stacked.astype(jnp.bfloat16)
    spectra = jnp.moveaxis(lax.map(channelize, jnp.arange(INPUTS, dtype=jnp.int32)), 0, 1)
    keep_float = channel_keep.astype(jnp.float32)
    counts = lax.optimization_barrier(jnp.sum(channel_keep.reshape(OUTCH, GROUP), axis=1))
    block_total = FINE // SUB

    def one_block(block_id):
        offset = (block_id * SUB).astype(jnp.int32)
        block_data = lax.dynamic_slice_in_dim(spectra, offset, SUB, 3).astype(jnp.float32)
        weights = lax.dynamic_slice_in_dim(keep_float, offset, SUB, 0)
        masked = block_data * weights
        left_real = masked[0].reshape(INPUTS, SPECTRA * SUB)
        left_imag = masked[1].reshape(INPUTS, SPECTRA * SUB)
        right_real = block_data[0].reshape(INPUTS, SPECTRA * SUB)
        right_imag = block_data[1].reshape(INPUTS, SPECTRA * SUB)
        vis_real = jnp.dot(left_real, right_real.T, precision=HIGHEST) + jnp.dot(left_imag, right_imag.T, precision=HIGHEST)
        vis_imag = jnp.dot(left_imag, right_real.T, precision=HIGHEST) - jnp.dot(left_real, right_imag.T, precision=HIGHEST)
        channel = offset // GROUP
        total_norm = counts[channel].astype(jnp.float32) * SPECTRA
        return (jnp.stack([vis_real, vis_imag]) / total_norm).astype(jnp.bfloat16)
    block_parts = lax.map(one_block, jnp.arange(block_total, dtype=jnp.int32))
    visibilities = lax.optimization_barrier(jnp.sum(block_parts.astype(jnp.float32).reshape(OUTCH, block_total // OUTCH, 2, INPUTS, INPUTS), axis=1))
    spectra_float = spectra.astype(jnp.float32)
    fine_ids = jnp.arange(FINE, dtype=jnp.int32)

    def one_beam(delays):
        phase_turns = delays[:, None] * fine_ids[None, :] % FINE
        angles = phase_turns.astype(jnp.float32) * (2.0 * math.pi / FINE)
        cos_weight = lax.optimization_barrier(jnp.cos(angles).astype(jnp.bfloat16)).astype(jnp.float32)
        sin_weight = lax.optimization_barrier(jnp.sin(angles).astype(jnp.bfloat16)).astype(jnp.float32)
        volt_real = jnp.einsum('ik,isk->sk', cos_weight, spectra_float[0], precision=HIGHEST) + jnp.einsum('ik,isk->sk', sin_weight, spectra_float[1], precision=HIGHEST)
        volt_imag = jnp.einsum('ik,isk->sk', cos_weight, spectra_float[1], precision=HIGHEST) - jnp.einsum('ik,isk->sk', sin_weight, spectra_float[0], precision=HIGHEST)
        energy = lax.optimization_barrier(jnp.sum(volt_real * volt_real + volt_imag * volt_imag, axis=0))
        return energy * keep_float / (INPUTS * SPECTRA)
    beam_power = lax.map(one_beam, beam_delay)
    return (visibilities, beam_power)
```

```python
import functools
import math

import jax
import jax.numpy as jnp
import numpy as np
from jax import lax
from jax.experimental import pallas as pl
from jax.experimental.pallas import tpu as pltpu
from jax.sharding import PartitionSpec as P

INPUTS = 1024
FINE = 3456
OUTCH = 16
TAPS = 6
R1 = 27
R2 = 128
LANES = 128
ROWS = 16


def cmul(a, w):
    (ar, ai), (wr, wi) = a, w
    return (ar * wr - ai * wi, ar * wi + ai * wr)


def unit(num, den):
    a = -2.0 * math.pi * (num % den) / den
    return (math.cos(a), math.sin(a))


def twist(a, num, den):
    if num % den == 0:
        return a
    return cmul(a, unit(num, den))


def dft3(x0, x1, x2):
    half_root3 = math.sqrt(3.0) / 2.0
    sr, si = x1[0] + x2[0], x1[1] + x2[1]
    dr, di = (x1[0] - x2[0]) * half_root3, (x1[1] - x2[1]) * half_root3
    mr, mi = x0[0] - 0.5 * sr, x0[1] - 0.5 * si
    return ((x0[0] + sr, x0[1] + si), (mr + di, mi - dr), (mr - di, mi + dr))


def dft9(x):
    inner = [dft3(x[f], x[3 + f], x[6 + f]) for f in range(3)]
    out = [None] * 9
    for g in range(3):
        res = dft3(*[twist(inner[f][g], f * g, 9) for f in range(3)])
        for h in range(3):
            out[g + 3 * h] = res[h]
    return out


def channelize_kernel(groups, per, x_ref, taps_ref, mat_ref, factor_ref, out_ref, mid_ref):
    step = pl.program_id(0)
    block_rows = x_ref.shape[1]

    def row_group(r, carry):
        rows = pl.ds(pl.multiple_of(r * ROWS, ROWS), ROWS)
        into = pl.ds(pl.multiple_of(step * block_rows + r * ROWS, ROWS), ROWS)

        def branch(n1):
            parts = []
            for part in range(2):
                total = None
                for p in range(TAPS):
                    at = p * FINE + n1 * R2
                    term = (
                        x_ref[part, rows, at : at + R2].astype(jnp.float32)
                        * taps_ref[p : p + 1, n1 * R2 : (n1 + 1) * R2]
                    )
                    total = term if total is None else total + term
                parts.append(total)
            return tuple(parts)

        first = [[None] * 9 for _ in range(3)]
        for b in range(9):
            res = dft3(branch(b), branch(9 + b), branch(18 + b))
            for c in range(3):
                first[c][b] = twist(res[c], b * c, 27)
        for c in range(3):
            res = dft9(first[c])
            for d in range(9):
                k1 = c + 3 * d
                mid_ref[k1, into, 0:R2] = res[d][0].astype(jnp.bfloat16)
                mid_ref[k1, into, R2 : 2 * R2] = res[d][1].astype(jnp.bfloat16)
        return carry

    lax.fori_loop(0, block_rows // ROWS, row_group, 0)

    @pl.when(step == pl.num_programs(0) - 1)
    def _():
        factor = factor_ref[...]

        def outer(k1, carry):
            res = lax.dot_general(
                mat_ref[k1],
                mid_ref[k1],
                (((1,), (1,)), ((), ())),
                preferred_element_type=jnp.float32,
            )
            res = (res * factor).astype(jnp.bfloat16)
            for og in range(groups):
                out_ref[og, k1] = res[og * 2 * per : (og + 1) * 2 * per]
            return carry

        lax.fori_loop(0, R1, outer, 0)


def transform_table(groups, per):
    k1 = np.arange(R1)[:, None, None]
    k2 = np.arange(R2)[None, :, None]
    n2 = np.arange(R2)[None, None, :]
    angle = 2.0 * np.pi * ((n2 * (k1 + R1 * k2)) % FINE) / FINE
    cos, sin = np.cos(angle), np.sin(angle)
    real_rows = np.concatenate([cos, sin], axis=2)
    imag_rows = np.concatenate([-sin, cos], axis=2)
    table = np.stack([real_rows, imag_rows], axis=1)
    table = table.reshape(R1, 2, groups, per, 2 * R2).transpose(0, 2, 1, 3, 4)
    return table.reshape(R1, 2 * R2, 2 * R2).astype(np.float32)


def channelize(samples, filter_taps, station_flags, channel_keep, groups, per):
    inputs_dev = samples.shape[1]
    x = samples.reshape(2, inputs_dev, TAPS * FINE)
    keep = channel_keep.reshape(R2, R1).T.reshape(R1, groups, 1, per)
    keep = jnp.broadcast_to(keep, (R1, groups, 2, per)).reshape(R1, 2 * R2, 1)
    table = jnp.asarray(transform_table(groups, per).astype(jnp.bfloat16))
    table = table * keep.astype(jnp.bfloat16)
    factor = (station_flags.astype(jnp.float32) / math.sqrt(FINE))[None, :]
    block = 32
    return pl.pallas_call(
        functools.partial(channelize_kernel, groups, per),
        grid=(inputs_dev // block,),
        in_specs=[
            pl.BlockSpec((2, block, TAPS * FINE), lambda i: (0, i, 0)),
            pl.BlockSpec((TAPS, FINE), lambda i: (0, 0)),
            pl.BlockSpec((R1, 2 * R2, 2 * R2), lambda i: (0, 0, 0)),
            pl.BlockSpec((1, inputs_dev), lambda i: (0, 0)),
        ],
        out_specs=pl.BlockSpec((groups, R1, 2 * per, inputs_dev), lambda i: (0, 0, 0, 0)),
        out_shape=jax.ShapeDtypeStruct((groups, R1, 2 * per, inputs_dev), jnp.bfloat16),
        scratch_shapes=[pltpu.VMEM((R1, inputs_dev, 2 * R2), jnp.bfloat16)],
        compiler_params=pltpu.CompilerParams(vmem_limit_bytes=48 << 20),
        name="channelize",
    )(x, filter_taps, table, factor)


def beam_kernel(per, x_ref, c1_ref, s1_ref, c2_ref, s2_ref, out_ref, w_ref):
    spec_count = x_ref.shape[0]
    inputs_dev = x_ref.shape[-1]
    beams = c1_ref.shape[1]
    cols = spec_count * 2 * per
    lane = lax.broadcasted_iota(jnp.int32, (beams, cols), 1)
    within = lane % per
    is_real = (lane % (2 * per)) < per

    def one(k1, carry):
        c1, s1 = c1_ref[k1], s1_ref[k1]
        for q in range(per):
            c2, s2 = c2_ref[q], s2_ref[q]
            w_ref[q * 2 * beams : q * 2 * beams + beams] = (c1 * c2 - s1 * s2).astype(jnp.bfloat16)
            w_ref[q * 2 * beams + beams : (q + 1) * 2 * beams] = (s1 * c2 + c1 * s2).astype(
                jnp.bfloat16
            )
        x = x_ref[:, 0, k1].reshape(cols, inputs_dev)
        prod = lax.dot_general(
            w_ref[...], x, (((1,), (1,)), ((), ())), preferred_element_type=jnp.float32
        )
        with_cos = prod[0:beams]
        with_sin = prod[beams : 2 * beams]
        for q in range(1, per):
            here = within == q
            with_cos = jnp.where(here, prod[q * 2 * beams : q * 2 * beams + beams], with_cos)
            with_sin = jnp.where(
                here, prod[q * 2 * beams + beams : (q + 1) * 2 * beams], with_sin
            )
        ahead = pltpu.roll(with_sin, cols - per, 1)
        behind = pltpu.roll(with_sin, per, 1)
        out_ref[0, k1] = (with_cos + jnp.where(is_real, ahead, -behind)).astype(jnp.bfloat16)
        return carry

    lax.fori_loop(0, R1, one, 0)


def beams_of(turned, delays, k2_start, local, per):
    spec_count, _, _, _, inputs_dev = turned.shape
    beams = delays.shape[0]
    cols = spec_count * 2 * per
    ids1 = jnp.arange(R1, dtype=jnp.int32)[:, None, None]
    ids2 = (k2_start + jnp.arange(local * per, dtype=jnp.int32))[:, None, None]
    ang1 = (delays[None] * ids1 % FINE).astype(jnp.float32) * (2.0 * math.pi / FINE)
    ang2 = (delays[None] * ids2 % R2).astype(jnp.float32) * (2.0 * math.pi / R2)
    small = pl.BlockSpec((R1, beams, inputs_dev), lambda o: (0, 0, 0))
    large = pl.BlockSpec((per, beams, inputs_dev), lambda o: (o, 0, 0))
    return pl.pallas_call(
        functools.partial(beam_kernel, per),
        grid=(local,),
        in_specs=[
            pl.BlockSpec((spec_count, 1, R1, 2 * per, inputs_dev), lambda o: (0, o, 0, 0, 0)),
            small,
            small,
            large,
            large,
        ],
        out_specs=pl.BlockSpec((1, R1, beams, cols), lambda o: (o, 0, 0, 0)),
        out_shape=jax.ShapeDtypeStruct((local, R1, beams, cols), jnp.bfloat16),
        scratch_shapes=[pltpu.VMEM((per * 2 * beams, inputs_dev), jnp.bfloat16)],
        compiler_params=pltpu.CompilerParams(vmem_limit_bytes=48 << 20),
        cost_estimate=pl.CostEstimate(
            flops=int(6e9), bytes_accessed=20 << 20, transcendentals=0
        ),
        name="beams",
    )(turned, jnp.cos(ang1), jnp.sin(ang1), jnp.cos(ang2), jnp.sin(ang2))


def left_kernel(per, x_ref, out_ref):
    inputs_dev = x_ref.shape[-1]
    depth = R1 * 2 * per
    x = x_ref[0, 0].reshape(depth, inputs_dev).astype(jnp.float32)
    pairs = x.reshape(R1, 2, per, inputs_dev)
    turned = jnp.concatenate([pairs[:, 1:], -pairs[:, :1]], axis=1).reshape(depth, inputs_dev)
    out_ref[0, 0, 0:inputs_dev] = x.T.astype(jnp.bfloat16)
    out_ref[0, 0, inputs_dev : 2 * inputs_dev] = turned.T.astype(jnp.bfloat16)


def left_of(turned, per):
    spec_count, local, _, _, inputs_dev = turned.shape
    depth = R1 * 2 * per
    return pl.pallas_call(
        functools.partial(left_kernel, per),
        grid=(local, spec_count),
        in_specs=[
            pl.BlockSpec((1, 1, R1, 2 * per, inputs_dev), lambda o, s: (s, o, 0, 0, 0)),
        ],
        out_specs=pl.BlockSpec((1, 1, 2 * inputs_dev, depth), lambda o, s: (o, s, 0, 0)),
        out_shape=jax.ShapeDtypeStruct((local, spec_count, 2 * inputs_dev, depth), jnp.bfloat16),
        compiler_params=pltpu.CompilerParams(vmem_limit_bytes=32 << 20),
        cost_estimate=pl.CostEstimate(flops=int(2e9), bytes_accessed=10 << 20, transcendentals=0),
        name="left_side",
    )(turned)


def correlate_kernel(scale_ref, left_ref, right_ref, out_ref):
    inputs_dev = right_ref.shape[-1]
    spec_count, depth = left_ref.shape[1], left_ref.shape[3]
    total = jnp.zeros((2 * inputs_dev, inputs_dev), jnp.float32)
    for s in range(spec_count):
        total = total + jnp.dot(
            left_ref[0, s],
            right_ref[0, s, 0].reshape(depth, inputs_dev),
            preferred_element_type=jnp.float32,
        )
    total = (total * scale_ref[pl.program_id(0)]).astype(jnp.bfloat16)
    for part in range(2):
        for h in range(inputs_dev // LANES):
            out_ref[h, 0, part] = total[
                part * inputs_dev : (part + 1) * inputs_dev, h * LANES : (h + 1) * LANES
            ]


def correlate(scale, left, right):
    count, spec_count, local, _, rows, inputs_dev = right.shape
    halves = inputs_dev // LANES
    depth = left.shape[3]
    return pl.pallas_call(
        correlate_kernel,
        grid=(local, count),
        in_specs=[
            pl.BlockSpec(memory_space=pltpu.SMEM),
            pl.BlockSpec((1, spec_count, 2 * inputs_dev, depth), lambda o, j: (o, 0, 0, 0)),
            pl.BlockSpec(
                (1, spec_count, 1, R1, rows, inputs_dev), lambda o, j: (j, 0, o, 0, 0, 0)
            ),
        ],
        out_specs=pl.BlockSpec(
            (halves, 1, 2, inputs_dev, LANES), lambda o, j: (j, o, 0, 0, 0)
        ),
        out_shape=jax.ShapeDtypeStruct(
            (count * halves, local, 2, inputs_dev, LANES), jnp.bfloat16
        ),
        compiler_params=pltpu.CompilerParams(vmem_limit_bytes=48 << 20),
        name="correlate",
    )(scale, left, right)


def on_device(stn_count, tm_count, samples, filter_taps, station_flags, channel_keep, beam_delay):
    inputs_dev = samples.shape[1]
    fine_dev = FINE // tm_count
    k2_dev = R2 // tm_count
    per = min(R2 // OUTCH, k2_dev)
    groups = R2 // per
    local = groups // tm_count
    spec_all = tm_count * samples.shape[2]
    tm_index = lax.axis_index("tm")
    stn_index = lax.axis_index("stn")

    spectra = channelize(samples, filter_taps, station_flags, channel_keep, groups, per)
    spectra = spectra.reshape(tm_count, local, R1, 2 * per, inputs_dev)
    turned = lax.all_to_all(spectra, "tm", 0, 0, tiled=True)
    gathered = lax.all_gather(turned, "stn", axis=0, tiled=False)

    own_delays = lax.dynamic_slice_in_dim(beam_delay, stn_index * inputs_dev, inputs_dev, 1)
    volts = beams_of(turned, own_delays, tm_index * k2_dev, local, per)
    left = left_of(turned, per)
    volts = lax.psum_scatter(volts, "stn", scatter_dimension=2, tiled=True).astype(jnp.float32)
    beams_dev = volts.shape[2]
    energy = jnp.sum(
        (volts * volts).reshape(local, R1, beams_dev, spec_all * 2, per), axis=3
    )
    energy = energy.transpose(2, 0, 3, 1).reshape(beams_dev, fine_dev)
    keep_local = lax.dynamic_slice_in_dim(channel_keep, tm_index * fine_dev, fine_dev, 0)
    beam_power = energy * keep_local.astype(jnp.float32) / (INPUTS * spec_all)

    counts = jnp.sum(channel_keep.reshape(OUTCH, FINE // OUTCH), axis=1)
    first = (tm_index * fine_dev) // (FINE // OUTCH)
    local_counts = lax.dynamic_slice_in_dim(counts, first, local, 0)
    scale = 1.0 / (local_counts.astype(jnp.float32) * spec_all)
    parts = correlate(scale, left, gathered)
    cols = INPUTS // tm_count
    if cols != LANES:
        parts = parts.reshape(-1, local, 2, inputs_dev, LANES // cols, cols)
        parts = parts.transpose(0, 4, 1, 2, 3, 5).reshape(-1, local, 2, inputs_dev, cols)
    swapped = lax.all_to_all(parts, "tm", 0, 0, tiled=True)
    swapped = swapped.reshape(OUTCH, -1, 2, inputs_dev, cols).astype(jnp.float32)
    visibilities = jnp.sum(swapped, axis=1)
    return (visibilities, beam_power)


def solution(mesh):
    return jax.shard_map(
        functools.partial(on_device, mesh.shape["stn"], mesh.shape["tm"]),
        mesh=mesh,
        in_specs=(P(None, "stn", "tm", None), P(), P("stn"), P(), P()),
        out_specs=(P(None, None, "stn", "tm"), P("stn", "tm")),
        check_vma=False,
    )
```

```python
import functools
import math

import jax
import jax.numpy as jnp
import numpy as np
from jax import lax
from jax.experimental import pallas as pl
from jax.experimental.pallas import tpu as pltpu
from jax.sharding import PartitionSpec as P

INPUTS = 1024
FINE = 3456
OUTCH = 16
TAPS = 6
R1 = 27
R2 = 128
LANES = 128
ROWS = 16


def cmul(a, w):
    (ar, ai), (wr, wi) = a, w
    return (ar * wr - ai * wi, ar * wi + ai * wr)


def unit(num, den):
    a = -2.0 * math.pi * (num % den) / den
    return (math.cos(a), math.sin(a))


def twist(a, num, den):
    if num % den == 0:
        return a
    return cmul(a, unit(num, den))


def dft3(x0, x1, x2):
    half_root3 = math.sqrt(3.0) / 2.0
    sr, si = x1[0] + x2[0], x1[1] + x2[1]
    dr, di = (x1[0] - x2[0]) * half_root3, (x1[1] - x2[1]) * half_root3
    mr, mi = x0[0] - 0.5 * sr, x0[1] - 0.5 * si
    return ((x0[0] + sr, x0[1] + si), (mr + di, mi - dr), (mr - di, mi + dr))


def dft9(x):
    inner = [dft3(x[f], x[3 + f], x[6 + f]) for f in range(3)]
    out = [None] * 9
    for g in range(3):
        res = dft3(*[twist(inner[f][g], f * g, 9) for f in range(3)])
        for h in range(3):
            out[g + 3 * h] = res[h]
    return out


def channelize_kernel(groups, per, local, x_ref, taps_ref, mat_ref, factor_ref, *rest):
    out_refs, mid_ref = rest[:local], rest[local]
    step = pl.program_id(0)
    block_rows = x_ref.shape[1]

    def row_group(r, carry):
        rows = pl.ds(pl.multiple_of(r * ROWS, ROWS), ROWS)
        into = pl.ds(pl.multiple_of(step * block_rows + r * ROWS, ROWS), ROWS)

        def branch(n1):
            parts = []
            for part in range(2):
                total = None
                for p in range(TAPS):
                    at = p * FINE + n1 * R2
                    term = (
                        x_ref[part, rows, at : at + R2].astype(jnp.float32)
                        * taps_ref[p : p + 1, n1 * R2 : (n1 + 1) * R2]
                    )
                    total = term if total is None else total + term
                parts.append(total)
            return tuple(parts)

        first = [[None] * 9 for _ in range(3)]
        for b in range(9):
            res = dft3(branch(b), branch(9 + b), branch(18 + b))
            for c in range(3):
                first[c][b] = twist(res[c], b * c, 27)
        for c in range(3):
            res = dft9(first[c])
            for d in range(9):
                k1 = c + 3 * d
                mid_ref[k1, into, 0:R2] = res[d][0].astype(jnp.bfloat16)
                mid_ref[k1, into, R2 : 2 * R2] = res[d][1].astype(jnp.bfloat16)
        return carry

    lax.fori_loop(0, block_rows // ROWS, row_group, 0)

    @pl.when(step == pl.num_programs(0) - 1)
    def _():
        factor = factor_ref[...]

        def outer(k1, carry):
            res = lax.dot_general(
                mat_ref[k1],
                mid_ref[k1],
                (((1,), (1,)), ((), ())),
                preferred_element_type=jnp.float32,
            )
            res = (res * factor).astype(jnp.bfloat16)
            for og in range(groups):
                out_refs[og % local][og // local, k1] = res[og * 2 * per : (og + 1) * 2 * per]
            return carry

        lax.fori_loop(0, R1, outer, 0)


def transform_table(groups, per):
    k1 = np.arange(R1)[:, None, None]
    k2 = np.arange(R2)[None, :, None]
    n2 = np.arange(R2)[None, None, :]
    angle = 2.0 * np.pi * ((n2 * (k1 + R1 * k2)) % FINE) / FINE
    cos, sin = np.cos(angle), np.sin(angle)
    real_rows = np.concatenate([cos, sin], axis=2)
    imag_rows = np.concatenate([-sin, cos], axis=2)
    table = np.stack([real_rows, imag_rows], axis=1)
    table = table.reshape(R1, 2, groups, per, 2 * R2).transpose(0, 2, 1, 3, 4)
    return table.reshape(R1, 2 * R2, 2 * R2).astype(np.float32)


def channelize(samples, filter_taps, station_flags, channel_keep, groups, per, local):
    inputs_dev = samples.shape[1]
    x = samples.reshape(2, inputs_dev, TAPS * FINE)
    keep = channel_keep.reshape(R2, R1).T.reshape(R1, groups, 1, per)
    keep = jnp.broadcast_to(keep, (R1, groups, 2, per)).reshape(R1, 2 * R2, 1)
    table = jnp.asarray(transform_table(groups, per).astype(jnp.bfloat16))
    table = table * keep.astype(jnp.bfloat16)
    factor = (station_flags.astype(jnp.float32) / math.sqrt(FINE))[None, :]
    block = 32
    return pl.pallas_call(
        functools.partial(channelize_kernel, groups, per, local),
        grid=(inputs_dev // block,),
        in_specs=[
            pl.BlockSpec((2, block, TAPS * FINE), lambda i: (0, i, 0)),
            pl.BlockSpec((TAPS, FINE), lambda i: (0, 0)),
            pl.BlockSpec((R1, 2 * R2, 2 * R2), lambda i: (0, 0, 0)),
            pl.BlockSpec((1, inputs_dev), lambda i: (0, 0)),
        ],
        out_specs=[
            pl.BlockSpec((groups // local, R1, 2 * per, inputs_dev), lambda i: (0, 0, 0, 0))
        ]
        * local,
        out_shape=[
            jax.ShapeDtypeStruct((groups // local, R1, 2 * per, inputs_dev), jnp.bfloat16)
        ]
        * local,
        scratch_shapes=[pltpu.VMEM((R1, inputs_dev, 2 * R2), jnp.bfloat16)],
        compiler_params=pltpu.CompilerParams(vmem_limit_bytes=48 << 20),
        name="channelize",
    )(x, filter_taps, table, factor)


def beam_kernel(per, x_ref, c1_ref, s1_ref, c2_ref, s2_ref, out_ref, w_ref):
    spec_count = x_ref.shape[0]
    inputs_dev = x_ref.shape[-1]
    beams = c1_ref.shape[1]
    cols = spec_count * 2 * per
    lane = lax.broadcasted_iota(jnp.int32, (beams, cols), 1)
    within = lane % per
    is_real = (lane % (2 * per)) < per

    def one(k1, carry):
        c1, s1 = c1_ref[k1], s1_ref[k1]
        for q in range(per):
            c2, s2 = c2_ref[q], s2_ref[q]
            w_ref[q * 2 * beams : q * 2 * beams + beams] = (c1 * c2 - s1 * s2).astype(jnp.bfloat16)
            w_ref[q * 2 * beams + beams : (q + 1) * 2 * beams] = (s1 * c2 + c1 * s2).astype(
                jnp.bfloat16
            )
        x = x_ref[:, 0, k1].reshape(cols, inputs_dev)
        prod = lax.dot_general(
            w_ref[...], x, (((1,), (1,)), ((), ())), preferred_element_type=jnp.float32
        )
        with_cos = prod[0:beams]
        with_sin = prod[beams : 2 * beams]
        for q in range(1, per):
            here = within == q
            with_cos = jnp.where(here, prod[q * 2 * beams : q * 2 * beams + beams], with_cos)
            with_sin = jnp.where(
                here, prod[q * 2 * beams + beams : (q + 1) * 2 * beams], with_sin
            )
        ahead = pltpu.roll(with_sin, cols - per, 1)
        behind = pltpu.roll(with_sin, per, 1)
        out_ref[0, k1] = (with_cos + jnp.where(is_real, ahead, -behind)).astype(jnp.bfloat16)
        return carry

    lax.fori_loop(0, R1, one, 0)


def beams_of(turned, delays, k2_start, local, per):
    spec_count, _, _, _, inputs_dev = turned.shape
    beams = delays.shape[0]
    cols = spec_count * 2 * per
    ids1 = jnp.arange(R1, dtype=jnp.int32)[:, None, None]
    ids2 = (k2_start + jnp.arange(local * per, dtype=jnp.int32))[:, None, None]
    ang1 = (delays[None] * ids1 % FINE).astype(jnp.float32) * (2.0 * math.pi / FINE)
    ang2 = (delays[None] * ids2 % R2).astype(jnp.float32) * (2.0 * math.pi / R2)
    small = pl.BlockSpec((R1, beams, inputs_dev), lambda o: (0, 0, 0))
    large = pl.BlockSpec((per, beams, inputs_dev), lambda o: (o, 0, 0))
    return pl.pallas_call(
        functools.partial(beam_kernel, per),
        grid=(local,),
        in_specs=[
            pl.BlockSpec((spec_count, 1, R1, 2 * per, inputs_dev), lambda o: (0, o, 0, 0, 0)),
            small,
            small,
            large,
            large,
        ],
        out_specs=pl.BlockSpec((1, R1, beams, cols), lambda o: (o, 0, 0, 0)),
        out_shape=jax.ShapeDtypeStruct((local, R1, beams, cols), jnp.bfloat16),
        scratch_shapes=[pltpu.VMEM((per * 2 * beams, inputs_dev), jnp.bfloat16)],
        compiler_params=pltpu.CompilerParams(vmem_limit_bytes=48 << 20),
        cost_estimate=pl.CostEstimate(
            flops=int(6e9), bytes_accessed=20 << 20, transcendentals=0
        ),
        name="beams",
    )(turned, jnp.cos(ang1), jnp.sin(ang1), jnp.cos(ang2), jnp.sin(ang2))


def left_kernel(per, x_ref, out_ref):
    inputs_dev = x_ref.shape[-1]
    depth = R1 * 2 * per
    x = x_ref[0, 0].reshape(depth, inputs_dev).astype(jnp.float32)
    pairs = x.reshape(R1, 2, per, inputs_dev)
    turned = jnp.concatenate([pairs[:, 1:], -pairs[:, :1]], axis=1).reshape(depth, inputs_dev)
    out_ref[0, 0, 0:inputs_dev] = x.T.astype(jnp.bfloat16)
    out_ref[0, 0, inputs_dev : 2 * inputs_dev] = turned.T.astype(jnp.bfloat16)


def left_of(turned, per):
    spec_count, local, _, _, inputs_dev = turned.shape
    depth = R1 * 2 * per
    return pl.pallas_call(
        functools.partial(left_kernel, per),
        grid=(local, spec_count),
        in_specs=[
            pl.BlockSpec((1, 1, R1, 2 * per, inputs_dev), lambda o, s: (s, o, 0, 0, 0)),
        ],
        out_specs=pl.BlockSpec((1, 1, 2 * inputs_dev, depth), lambda o, s: (o, s, 0, 0)),
        out_shape=jax.ShapeDtypeStruct((local, spec_count, 2 * inputs_dev, depth), jnp.bfloat16),
        compiler_params=pltpu.CompilerParams(vmem_limit_bytes=32 << 20),
        cost_estimate=pl.CostEstimate(flops=int(2e9), bytes_accessed=10 << 20, transcendentals=0),
        name="left_side",
    )(turned)


def correlate_kernel(scale_ref, left_ref, right_ref, out_ref):
    inputs_dev = right_ref.shape[-1]
    spec_count, depth = left_ref.shape[1], left_ref.shape[3]
    total = jnp.zeros((2 * inputs_dev, inputs_dev), jnp.float32)
    for s in range(spec_count):
        total = total + jnp.dot(
            left_ref[0, s],
            right_ref[0, s, 0].reshape(depth, inputs_dev),
            preferred_element_type=jnp.float32,
        )
    total = (total * scale_ref[pl.program_id(0)]).astype(jnp.bfloat16)
    for part in range(2):
        for h in range(inputs_dev // LANES):
            out_ref[h, 0, part] = total[
                part * inputs_dev : (part + 1) * inputs_dev, h * LANES : (h + 1) * LANES
            ]


def correlate(scale, left, right):
    count, spec_count, local, _, rows, inputs_dev = right.shape
    halves = inputs_dev // LANES
    depth = left.shape[3]
    return pl.pallas_call(
        correlate_kernel,
        grid=(local, count),
        in_specs=[
            pl.BlockSpec(memory_space=pltpu.SMEM),
            pl.BlockSpec((1, spec_count, 2 * inputs_dev, depth), lambda o, j: (o, 0, 0, 0)),
            pl.BlockSpec(
                (1, spec_count, 1, R1, rows, inputs_dev), lambda o, j: (j, 0, o, 0, 0, 0)
            ),
        ],
        out_specs=pl.BlockSpec(
            (halves, 1, 2, inputs_dev, LANES), lambda o, j: (j, o, 0, 0, 0)
        ),
        out_shape=jax.ShapeDtypeStruct(
            (count * halves, local, 2, inputs_dev, LANES), jnp.bfloat16
        ),
        compiler_params=pltpu.CompilerParams(vmem_limit_bytes=48 << 20),
        name="correlate",
    )(scale, left, right)


def widen_kernel(*refs):
    out_ref = refs[-1]
    for o, ref in enumerate(refs[:-1]):
        out_ref[o] = ref[0].astype(jnp.float32)


def widen(parts):
    count, _, rows, cols = parts[0].shape
    local = len(parts)
    return pl.pallas_call(
        widen_kernel,
        grid=(count,),
        in_specs=[pl.BlockSpec((1, 2, rows, cols), lambda i: (i, 0, 0, 0))] * local,
        out_specs=pl.BlockSpec((local, 2, rows, cols), lambda i: (i, 0, 0, 0)),
        out_shape=jax.ShapeDtypeStruct((count * local, 2, rows, cols), jnp.float32),
        name="widen",
    )(*parts)


def on_device(stn_count, tm_count, samples, filter_taps, station_flags, channel_keep, beam_delay):
    inputs_dev = samples.shape[1]
    fine_dev = FINE // tm_count
    k2_dev = R2 // tm_count
    per = min(R2 // OUTCH, k2_dev)
    groups = R2 // per
    local = groups // tm_count
    spec_all = tm_count * samples.shape[2]
    tm_index = lax.axis_index("tm")
    stn_index = lax.axis_index("stn")

    spectra = channelize(
        samples, filter_taps, station_flags, channel_keep, groups, per, local
    )
    own_delays = lax.dynamic_slice_in_dim(beam_delay, stn_index * inputs_dev, inputs_dev, 1)
    counts = jnp.sum(channel_keep.reshape(OUTCH, FINE // OUTCH), axis=1)
    first = (tm_index * fine_dev) // (FINE // OUTCH)
    local_counts = lax.dynamic_slice_in_dim(counts, first, local, 0)
    scale = 1.0 / (local_counts.astype(jnp.float32) * spec_all)
    cols = INPUTS // tm_count

    turned, gathered, volts, vis = [], [], [], []
    for o in range(local):
        turned.append(lax.all_to_all(spectra[o][:, None], "tm", 0, 0, tiled=True))
        gathered.append(lax.all_gather(turned[o], "stn", axis=0, tiled=False))
    for o in range(local):
        left = left_of(turned[o], per)
        volts.append(
            beams_of(turned[o], own_delays, tm_index * k2_dev + o * per, 1, per)
        )
        parts = correlate(scale[o : o + 1], left, gathered[o])
        if cols != LANES:
            parts = parts.reshape(-1, 2, inputs_dev, LANES // cols, cols)
            parts = parts.transpose(0, 3, 1, 2, 4)
        parts = parts.reshape(tm_count, 2, inputs_dev, cols)
        vis.append(lax.all_to_all(parts, "tm", 0, 0, tiled=True))
    if tm_count * local == OUTCH and cols == LANES:
        visibilities = widen(vis)
    else:
        swapped = jnp.stack(vis, axis=1).reshape(OUTCH, -1, 2, inputs_dev, cols)
        visibilities = jnp.sum(swapped.astype(jnp.float32), axis=1)

    volts = jnp.concatenate(volts, axis=0)
    volts = lax.psum_scatter(volts, "stn", scatter_dimension=2, tiled=True).astype(jnp.float32)
    beams_dev = volts.shape[2]
    energy = jnp.sum(
        (volts * volts).reshape(local, R1, beams_dev, spec_all * 2, per), axis=3
    )
    energy = energy.transpose(2, 0, 3, 1).reshape(beams_dev, fine_dev)
    keep_local = lax.dynamic_slice_in_dim(channel_keep, tm_index * fine_dev, fine_dev, 0)
    beam_power = energy * keep_local.astype(jnp.float32) / (INPUTS * spec_all)
    return (visibilities, beam_power)


def solution(mesh):
    return jax.shard_map(
        functools.partial(on_device, mesh.shape["stn"], mesh.shape["tm"]),
        mesh=mesh,
        in_specs=(P(None, "stn", "tm", None), P(), P("stn"), P(), P()),
        out_specs=(P(None, None, "stn", "tm"), P("stn", "tm")),
        check_vma=False,
    )
```

```python
import functools
import math

import jax
import jax.numpy as jnp
import numpy as np
from jax import lax
from jax.experimental import pallas as pl
from jax.experimental.pallas import tpu as pltpu
from jax.sharding import PartitionSpec as P

INPUTS = 1024
FINE = 3456
OUTCH = 16
TAPS = 6
R1 = 27
R2 = 128
LANES = 128
PIECES = (14, 13)
ROWS = 16


def cmul(a, w):
    (ar, ai), (wr, wi) = a, w
    return (ar * wr - ai * wi, ar * wi + ai * wr)


def unit(num, den):
    a = -2.0 * math.pi * (num % den) / den
    return (math.cos(a), math.sin(a))


def twist(a, num, den):
    if num % den == 0:
        return a
    return cmul(a, unit(num, den))


def dft3(x0, x1, x2):
    half_root3 = math.sqrt(3.0) / 2.0
    sr, si = x1[0] + x2[0], x1[1] + x2[1]
    dr, di = (x1[0] - x2[0]) * half_root3, (x1[1] - x2[1]) * half_root3
    mr, mi = x0[0] - 0.5 * sr, x0[1] - 0.5 * si
    return ((x0[0] + sr, x0[1] + si), (mr + di, mi - dr), (mr - di, mi + dr))


def dft9(x):
    inner = [dft3(x[f], x[3 + f], x[6 + f]) for f in range(3)]
    out = [None] * 9
    for g in range(3):
        res = dft3(*[twist(inner[f][g], f * g, 9) for f in range(3)])
        for h in range(3):
            out[g + 3 * h] = res[h]
    return out


def channelize_kernel(groups, per, local, x_ref, taps_ref, mat_ref, factor_ref, *rest):
    out_refs, mid_ref = rest[:-1], rest[-1]
    step = pl.program_id(0)
    block_rows = x_ref.shape[1]

    def row_group(r, carry):
        rows = pl.ds(pl.multiple_of(r * ROWS, ROWS), ROWS)
        into = pl.ds(pl.multiple_of(step * block_rows + r * ROWS, ROWS), ROWS)

        def branch(n1):
            parts = []
            for part in range(2):
                total = None
                for p in range(TAPS):
                    at = p * FINE + n1 * R2
                    term = (
                        x_ref[part, rows, at : at + R2].astype(jnp.float32)
                        * taps_ref[p : p + 1, n1 * R2 : (n1 + 1) * R2]
                    )
                    total = term if total is None else total + term
                parts.append(total)
            return tuple(parts)

        first = [[None] * 9 for _ in range(3)]
        for b in range(9):
            res = dft3(branch(b), branch(9 + b), branch(18 + b))
            for c in range(3):
                first[c][b] = twist(res[c], b * c, 27)
        for c in range(3):
            res = dft9(first[c])
            for d in range(9):
                k1 = c + 3 * d
                mid_ref[k1, into, 0:R2] = res[d][0].astype(jnp.bfloat16)
                mid_ref[k1, into, R2 : 2 * R2] = res[d][1].astype(jnp.bfloat16)
        return carry

    lax.fori_loop(0, block_rows // ROWS, row_group, 0)

    @pl.when(step == pl.num_programs(0) - 1)
    def _():
        factor = factor_ref[...]

        def outer(piece, start, k1, carry):
            res = lax.dot_general(
                mat_ref[k1],
                mid_ref[k1],
                (((1,), (1,)), ((), ())),
                preferred_element_type=jnp.float32,
            )
            res = (res * factor).astype(jnp.bfloat16)
            for og in range(groups):
                out_refs[og % local * len(PIECES) + piece][og // local, k1 - start] = res[
                    og * 2 * per : (og + 1) * 2 * per
                ]
            return carry

        start = 0
        for piece, size in enumerate(PIECES):
            lax.fori_loop(start, start + size, functools.partial(outer, piece, start), 0)
            start += size


def transform_table(groups, per):
    k1 = np.arange(R1)[:, None, None]
    k2 = np.arange(R2)[None, :, None]
    n2 = np.arange(R2)[None, None, :]
    angle = 2.0 * np.pi * ((n2 * (k1 + R1 * k2)) % FINE) / FINE
    cos, sin = np.cos(angle), np.sin(angle)
    real_rows = np.concatenate([cos, sin], axis=2)
    imag_rows = np.concatenate([-sin, cos], axis=2)
    table = np.stack([real_rows, imag_rows], axis=1)
    table = table.reshape(R1, 2, groups, per, 2 * R2).transpose(0, 2, 1, 3, 4)
    return table.reshape(R1, 2 * R2, 2 * R2).astype(np.float32)


def channelize(samples, filter_taps, station_flags, channel_keep, groups, per, local):
    inputs_dev = samples.shape[1]
    x = samples.reshape(2, inputs_dev, TAPS * FINE)
    keep = channel_keep.reshape(R2, R1).T.reshape(R1, groups, 1, per)
    keep = jnp.broadcast_to(keep, (R1, groups, 2, per)).reshape(R1, 2 * R2, 1)
    table = jnp.asarray(transform_table(groups, per).astype(jnp.bfloat16))
    table = table * keep.astype(jnp.bfloat16)
    factor = (station_flags.astype(jnp.float32) / math.sqrt(FINE))[None, :]
    block = 32
    return pl.pallas_call(
        functools.partial(channelize_kernel, groups, per, local),
        grid=(inputs_dev // block,),
        in_specs=[
            pl.BlockSpec((2, block, TAPS * FINE), lambda i: (0, i, 0)),
            pl.BlockSpec((TAPS, FINE), lambda i: (0, 0)),
            pl.BlockSpec((R1, 2 * R2, 2 * R2), lambda i: (0, 0, 0)),
            pl.BlockSpec((1, inputs_dev), lambda i: (0, 0)),
        ],
        out_specs=[
            pl.BlockSpec((groups // local, size, 2 * per, inputs_dev), lambda i: (0, 0, 0, 0))
            for size in PIECES
        ]
        * local,
        out_shape=[
            jax.ShapeDtypeStruct((groups // local, size, 2 * per, inputs_dev), jnp.bfloat16)
            for size in PIECES
        ]
        * local,
        scratch_shapes=[pltpu.VMEM((R1, inputs_dev, 2 * R2), jnp.bfloat16)],
        compiler_params=pltpu.CompilerParams(vmem_limit_bytes=48 << 20),
        name="channelize",
    )(x, filter_taps, table, factor)


def beam_kernel(per, base_ref, *refs):
    x_refs, (out_ref, w_ref, step_ref) = refs[: len(PIECES)], refs[len(PIECES) :]
    spec_count = x_refs[0].shape[0]
    inputs_dev = x_refs[0].shape[-1]
    beams = base_ref.shape[1]
    cols = spec_count * 2 * per
    lane = lax.broadcasted_iota(jnp.int32, (beams, cols), 1)
    within = lane % per
    is_real = (lane % (2 * per)) < per

    c2, s2 = base_ref[4], base_ref[5]
    for q in range(per):
        step_ref[2 * q], step_ref[2 * q + 1] = c2, s2
        c2, s2 = cmul((c2, s2), (base_ref[2], base_ref[3]))
    step_ref[2 * per] = jnp.ones((beams, inputs_dev), jnp.float32)
    step_ref[2 * per + 1] = jnp.zeros((beams, inputs_dev), jnp.float32)

    def one(x_ref, start, k1, carry):
        c1, s1 = step_ref[2 * per], step_ref[2 * per + 1]
        for q in range(per):
            cos, sin = cmul((c1, s1), (step_ref[2 * q], step_ref[2 * q + 1]))
            w_ref[q * 2 * beams : q * 2 * beams + beams] = cos.astype(jnp.bfloat16)
            w_ref[q * 2 * beams + beams : (q + 1) * 2 * beams] = sin.astype(jnp.bfloat16)
        c1, s1 = cmul((c1, s1), (base_ref[0], base_ref[1]))
        step_ref[2 * per], step_ref[2 * per + 1] = c1, s1
        x = x_ref[:, 0, k1 - start].reshape(cols, inputs_dev)
        prod = lax.dot_general(
            w_ref[...], x, (((1,), (1,)), ((), ())), preferred_element_type=jnp.float32
        )
        with_cos = prod[0:beams]
        with_sin = prod[beams : 2 * beams]
        for q in range(1, per):
            here = within == q
            with_cos = jnp.where(here, prod[q * 2 * beams : q * 2 * beams + beams], with_cos)
            with_sin = jnp.where(
                here, prod[q * 2 * beams + beams : (q + 1) * 2 * beams], with_sin
            )
        ahead = pltpu.roll(with_sin, cols - per, 1)
        behind = pltpu.roll(with_sin, per, 1)
        out_ref[0, k1] = (with_cos + jnp.where(is_real, ahead, -behind)).astype(jnp.bfloat16)
        return carry

    start = 0
    for x_ref, size in zip(x_refs, PIECES):
        lax.fori_loop(start, start + size, functools.partial(one, x_ref, start), 0)
        start += size


def beams_of(turned, delays, k2_start, per):
    spec_count, inputs_dev = turned[0].shape[0], turned[0].shape[-1]
    beams = delays.shape[0]
    cols = spec_count * 2 * per
    turns = jnp.stack([delays, delays * R1 % FINE, (delays * k2_start % R2) * R1])
    angles = turns.astype(jnp.float32) * (2.0 * math.pi / FINE)
    base = jnp.stack([jnp.cos(angles), jnp.sin(angles)], axis=1)
    base = base.reshape(6, beams, inputs_dev)
    return pl.pallas_call(
        functools.partial(beam_kernel, per),
        out_shape=jax.ShapeDtypeStruct((1, R1, beams, cols), jnp.bfloat16),
        scratch_shapes=[
            pltpu.VMEM((per * 2 * beams, inputs_dev), jnp.bfloat16),
            pltpu.VMEM((2 * per + 2, beams, inputs_dev), jnp.float32),
        ],
        compiler_params=pltpu.CompilerParams(vmem_limit_bytes=32 << 20),
        cost_estimate=pl.CostEstimate(
            flops=int(6e9), bytes_accessed=10 << 20, transcendentals=0
        ),
        name="beams",
    )(base, *turned)


def left_kernel(per, x_ref, out_ref):
    inputs_dev = x_ref.shape[-1]
    size = x_ref.shape[2]
    depth = size * 2 * per
    x = x_ref[0, 0].reshape(depth, inputs_dev).astype(jnp.float32)
    pairs = x.reshape(size, 2, per, inputs_dev)
    turned = jnp.concatenate([pairs[:, 1:], -pairs[:, :1]], axis=1).reshape(depth, inputs_dev)
    out_ref[0, 0, 0:inputs_dev] = x.T.astype(jnp.bfloat16)
    out_ref[0, 0, inputs_dev : 2 * inputs_dev] = turned.T.astype(jnp.bfloat16)


def left_of(turned, per):
    spec_count, local, size, _, inputs_dev = turned.shape
    depth = size * 2 * per
    return pl.pallas_call(
        functools.partial(left_kernel, per),
        grid=(local, spec_count),
        in_specs=[
            pl.BlockSpec((1, 1, size, 2 * per, inputs_dev), lambda o, s: (s, o, 0, 0, 0)),
        ],
        out_specs=pl.BlockSpec((1, 1, 2 * inputs_dev, depth), lambda o, s: (o, s, 0, 0)),
        out_shape=jax.ShapeDtypeStruct((local, spec_count, 2 * inputs_dev, depth), jnp.bfloat16),
        compiler_params=pltpu.CompilerParams(vmem_limit_bytes=32 << 20),
        cost_estimate=pl.CostEstimate(flops=int(5e8), bytes_accessed=3 << 20, transcendentals=0),
        name="left_side",
    )(turned)


def correlate_kernel(scale_ref, *refs):
    count = len(PIECES)
    lefts, rights, out_ref = refs[:count], refs[count : 2 * count], refs[-1]
    inputs_dev = rights[0].shape[-1]
    spec_count = lefts[0].shape[1]
    total = jnp.zeros((2 * inputs_dev, inputs_dev), jnp.float32)
    for left_ref, right_ref in zip(lefts, rights):
        depth = left_ref.shape[3]
        for s in range(spec_count):
            total = total + jnp.dot(
                left_ref[0, s],
                right_ref[0, s, 0].reshape(depth, inputs_dev),
                preferred_element_type=jnp.float32,
            )
    total = (total * scale_ref[0]).astype(jnp.bfloat16)
    for part in range(2):
        for h in range(inputs_dev // LANES):
            out_ref[h, part] = total[
                part * inputs_dev : (part + 1) * inputs_dev, h * LANES : (h + 1) * LANES
            ]


def correlate(scale, lefts, rights):
    count, spec_count, _, _, rows, inputs_dev = rights[0].shape
    halves = inputs_dev // LANES
    return pl.pallas_call(
        correlate_kernel,
        grid=(count,),
        in_specs=[pl.BlockSpec(memory_space=pltpu.SMEM)]
        + [pl.BlockSpec(left.shape, lambda j: (0, 0, 0, 0)) for left in lefts]
        + [
            pl.BlockSpec((1,) + right.shape[1:], lambda j: (j, 0, 0, 0, 0, 0))
            for right in rights
        ],
        out_specs=pl.BlockSpec((halves, 2, inputs_dev, LANES), lambda j: (j, 0, 0, 0)),
        out_shape=jax.ShapeDtypeStruct((count * halves, 2, inputs_dev, LANES), jnp.bfloat16),
        compiler_params=pltpu.CompilerParams(vmem_limit_bytes=48 << 20),
        cost_estimate=pl.CostEstimate(
            flops=int(7e9), bytes_accessed=12 << 20, transcendentals=0
        ),
        name="correlate",
    )(scale, *lefts, *rights)


def widen_kernel(*refs):
    out_ref = refs[-1]
    for o, ref in enumerate(refs[:-1]):
        out_ref[o] = ref[0].astype(jnp.float32)


def widen(parts):
    count, _, rows, cols = parts[0].shape
    local = len(parts)
    return pl.pallas_call(
        widen_kernel,
        grid=(count,),
        in_specs=[pl.BlockSpec((1, 2, rows, cols), lambda i: (i, 0, 0, 0))] * local,
        out_specs=pl.BlockSpec((local, 2, rows, cols), lambda i: (i, 0, 0, 0)),
        out_shape=jax.ShapeDtypeStruct((count * local, 2, rows, cols), jnp.float32),
        name="widen",
    )(*parts)


def on_device(stn_count, tm_count, samples, filter_taps, station_flags, channel_keep, beam_delay):
    inputs_dev = samples.shape[1]
    fine_dev = FINE // tm_count
    k2_dev = R2 // tm_count
    per = min(R2 // OUTCH, k2_dev)
    groups = R2 // per
    local = groups // tm_count
    spec_all = tm_count * samples.shape[2]
    tm_index = lax.axis_index("tm")
    stn_index = lax.axis_index("stn")

    spectra = channelize(
        samples, filter_taps, station_flags, channel_keep, groups, per, local
    )
    own_delays = lax.dynamic_slice_in_dim(beam_delay, stn_index * inputs_dev, inputs_dev, 1)
    counts = jnp.sum(channel_keep.reshape(OUTCH, FINE // OUTCH), axis=1)
    first = (tm_index * fine_dev) // (FINE // OUTCH)
    local_counts = lax.dynamic_slice_in_dim(counts, first, local, 0)
    scale = 1.0 / (local_counts.astype(jnp.float32) * spec_all)
    cols = INPUTS // tm_count

    turned, gathered, volts, vis = [], [], [], []
    for o in range(local):
        own = spectra[o * len(PIECES) : (o + 1) * len(PIECES)]
        turned.append([lax.all_to_all(x[:, None], "tm", 0, 0, tiled=True) for x in own])
        gathered.append([lax.all_gather(x, "stn", axis=0, tiled=False) for x in turned[o]])
    for o in range(local):
        lefts = [left_of(x, per) for x in turned[o]]
        volts.append(beams_of(turned[o], own_delays, tm_index * k2_dev + o * per, per))
        parts = correlate(scale[o : o + 1], lefts, gathered[o])
        if cols != LANES:
            parts = parts.reshape(-1, 2, inputs_dev, LANES // cols, cols)
            parts = parts.transpose(0, 3, 1, 2, 4)
        parts = parts.reshape(tm_count, 2, inputs_dev, cols)
        vis.append(lax.all_to_all(parts, "tm", 0, 0, tiled=True))
    if tm_count * local == OUTCH and cols == LANES:
        visibilities = widen(vis)
    else:
        swapped = jnp.stack(vis, axis=1).reshape(OUTCH, -1, 2, inputs_dev, cols)
        visibilities = jnp.sum(swapped.astype(jnp.float32), axis=1)

    volts = jnp.concatenate(volts, axis=0)
    volts = lax.psum_scatter(volts, "stn", scatter_dimension=2, tiled=True).astype(jnp.float32)
    beams_dev = volts.shape[2]
    energy = jnp.sum(
        (volts * volts).reshape(local, R1, beams_dev, spec_all * 2, per), axis=3
    )
    energy = energy.transpose(2, 0, 3, 1).reshape(beams_dev, fine_dev)
    keep_local = lax.dynamic_slice_in_dim(channel_keep, tm_index * fine_dev, fine_dev, 0)
    beam_power = energy * keep_local.astype(jnp.float32) / (INPUTS * spec_all)
    return (visibilities, beam_power)


def solution(mesh):
    return jax.shard_map(
        functools.partial(on_device, mesh.shape["stn"], mesh.shape["tm"]),
        mesh=mesh,
        in_specs=(P(None, "stn", "tm", None), P(), P("stn"), P(), P()),
        out_specs=(P(None, None, "stn", "tm"), P("stn", "tm")),
        check_vma=False,
    )
```
